256 devices in a mesh: seq: 32 (over z_lo, x, core), dp: 8 (over y, z_hi).
Axes of the slice: x: 4, y: 4, z: 8 (z_hi: 2, z_lo: 4; z = z_hi * 4 + z_lo), core: 2. Of those that a mesh axis runs over, the one named last changes fastest.
Arguments:
- features: bfloat16 [64, 4096, 768], P('dp', 'seq'), may hold values from -6 to 6
- kernel: bfloat16 [3, 768, 768], replicated, may hold values from -0.125 to 0.125
- cotangent: bfloat16 [64, 4096, 768], P('dp', 'seq'), may hold values from -6 to 6
Outputs:
- outputs: bfloat16 [64, 4096, 768], P('dp', 'seq')
- input_grad: bfloat16 [64, 4096, 768], P('dp', 'seq')
- weight_grad: float32 [3, 768, 768], P(None, 'seq', 'dp')
The draws below stay inside these ranges and needn't reach their ends.
All inputs are finite; a program needn't handle non-finite values.
Results may differ from the reference program's by a relative error of at most 0.0034.
Values may be sent and summed in bfloat16 or wider, within the bound.
A program may use at most 64 MiB of HBM per device.

```python
import math
import jax
import jax.numpy as jnp
from jax import lax

C = 768
DILATION_STEP = 64
BATCH = 64
SEQUENCE_BINS = 4096


def block_levels(own_key, dims, cuts, least, high):
    factor_of = 1.0
    for dim, blocks in cuts:
        draws = jax.random.uniform(jax.random.fold_in(jax.random.fold_in(own_key, 6), dim), (blocks,), jnp.float32, least / len(cuts), high / len(cuts))
        factor_of = factor_of * jnp.repeat(jnp.exp(draws), dims[dim] // blocks).reshape((-1,) + (1,) * (len(dims) - 1 - dim))
    return factor_of


def normal_values(rng, shape, spread, bound, split=(), held_as=jnp.bfloat16):
    values = jax.random.normal(rng, shape, jnp.float32) * spread
    if len(split) > 0:
        values = block_levels(rng, shape, split, -0.22, 0.18) * values
    return jnp.clip(values, min=-bound, max=bound).astype(held_as)


def setup_inputs(seed: int = 0) -> dict:
    keys = jax.random.split(jax.random.key(seed), 4)
    return {
        "features": normal_values(keys[0], (BATCH, SEQUENCE_BINS, C), 1.0, 6.0, ((0, 8), (1, 32))),
        "kernel": normal_values(keys[1], (3, C, C), (3 * C) ** -0.5, 0.125),
        "cotangent": normal_values(keys[2], (BATCH, SEQUENCE_BINS, C), 1.0, 6.0, ((0, 8), (1, 32))),
    }


def reference(features, kernel, cotangent):

    def one_sequence(totals, sequence_pair):
        inputs, incoming_gradient = sequence_pair
        widened = inputs.astype(jnp.float32)
        gelu_output = jax.nn.gelu(widened).astype(jnp.bfloat16)
        padded_gelu_rows = jnp.pad(gelu_output, ((DILATION_STEP, DILATION_STEP), (0, 0)))
        padded_upstream_rows = jnp.pad(incoming_gradient, ((DILATION_STEP, DILATION_STEP), (0, 0)))
        conv_sum = jnp.zeros((SEQUENCE_BINS, C), jnp.float32)
        back_sum = jnp.zeros((SEQUENCE_BINS, C), jnp.float32)
        new_totals = []
        for kernel_tap_index in range(3):
            offset_rows = padded_gelu_rows[kernel_tap_index * DILATION_STEP:kernel_tap_index * DILATION_STEP + SEQUENCE_BINS]
            conv_sum = conv_sum + jnp.dot(offset_rows, kernel[kernel_tap_index], preferred_element_type=jnp.float32)
            trailing_rows = padded_upstream_rows[(2 - kernel_tap_index) * DILATION_STEP:(2 - kernel_tap_index) * DILATION_STEP + SEQUENCE_BINS]
            back_sum = back_sum + jnp.dot(trailing_rows, kernel[kernel_tap_index].T, preferred_element_type=jnp.float32)
            new_totals.append(totals[kernel_tap_index] + jnp.dot(offset_rows.T, incoming_gradient, preferred_element_type=jnp.float32))
        outputs = (widened + conv_sum).astype(jnp.bfloat16)
        unused, pullback = jax.vjp(jax.nn.gelu, widened)
        slope_term = pullback(back_sum)[0]
        input_grad = (incoming_gradient.astype(jnp.float32) + slope_term).astype(jnp.bfloat16)
        return (jnp.stack(new_totals), (outputs, input_grad))
    totals, (outputs, input_grad) = lax.scan(one_sequence, jnp.zeros((3, C, C), jnp.float32), (features, cotangent))
    return (outputs, input_grad, totals * (1.0 / math.sqrt(BATCH * SEQUENCE_BINS)))
```

```python
import functools
import math

import jax
import jax.numpy as jnp
from jax import lax
from jax.experimental import pallas as pl
from jax.experimental.pallas import tpu as pltpu
from jax.sharding import PartitionSpec as P

MESH = pl.DeviceIdType.MESH
BF16 = jnp.bfloat16
F32 = jnp.float32
SEQS = 8
HALF = 64
WIDTH = 768
ROWS = SEQS * HALF
TILE = 256
TILES = WIDTH // TILE
ROOT = math.sqrt(2.0 / math.pi)
CUBIC = 0.044715
FACTOR = 1.0 / math.sqrt(64 * 4096)
FULL_TILE = (0, 2, 3, 5)
SHARED_TILE = (1, 1, 4, 4)


def dot(a, b):
    return lax.dot_general(a, b, (((1,), (0,)), ((), ())), preferred_element_type=F32)


def dot_t(a, b):
    return lax.dot_general(a, b, (((1,), (1,)), ((), ())), preferred_element_type=F32)


def kernel(
    f_hbm, k_hbm, c_hbm, out_hbm, gin_hbm, wg_ref,
    f_v, c_v, k_v, a_v, at_v, d_v, c_halo, a_halo, conv, back, o_v, g_v,
    part, mate_part, ys, yr, xs, xr, zs, zr,
    in_sem, out_sem, halo_s, halo_r, core_s, core_r, y_s, y_r, x_s, x_r, z_s, z_r,
):
    s = lax.axis_index("seq")
    d = lax.axis_index("dp")
    core = lax.rem(s, 2)
    x = lax.rem(s // 2, 4)
    z_lo = s // 8
    y = d // 2
    z_hi = lax.rem(d, 2)
    z = z_hi * 4 + z_lo
    left = lax.rem(s + 31, 32)
    right = lax.rem(s + 1, 32)
    mate = s + 1 - 2 * core

    def y_partner(k):
        return {"seq": s, "dp": lax.rem(y + k, 4) * 2 + z_hi}

    def x_partner(k):
        return {"seq": (z_lo * 4 + lax.rem(x + k, 4)) * 2 + core, "dp": d}

    def z_partner(k):
        other = lax.rem(z + k, 8)
        return {"seq": (lax.rem(other, 4) * 4 + x) * 2 + core, "dp": y * 2 + other // 4}

    loads = []
    for half in range(2):
        rows = pl.ds(half * HALF, HALF)
        loads.append(pltpu.make_async_copy(f_hbm.at[:, rows, :], f_v.at[half], in_sem.at[half]))
    for half in range(2):
        rows = pl.ds(half * HALF, HALF)
        loads.append(pltpu.make_async_copy(c_hbm.at[:, rows, :], c_v.at[half], in_sem.at[2 + half]))
    loads.append(pltpu.make_async_copy(k_hbm, k_v, in_sem.at[4]))
    for load in loads:
        load.start()

    barrier = pltpu.get_barrier_semaphore()
    partners = [{"seq": left, "dp": d}, {"seq": right, "dp": d}]
    partners += [y_partner(k) for k in range(1, 4)]
    partners += [x_partner(k) for k in range(1, 4)]
    partners += [z_partner(k) for k in range(1, 8)]
    for partner in partners:
        pl.semaphore_signal(barrier, inc=1, device_id=partner, device_id_type=MESH)
    pl.semaphore_wait(barrier, len(partners))

    def remote(src, dst, send_sem, recv_sem, device):
        return pltpu.make_async_remote_copy(
            src_ref=src, dst_ref=dst, send_sem=send_sem, recv_sem=recv_sem,
            device_id=device, device_id_type=MESH,
        )

    def halo(i, src, dst):
        to_right = remote(src(1), dst.at[0], halo_s.at[2 * i], halo_r.at[2 * i], {"seq": right, "dp": d})
        to_left = remote(src(0), dst.at[1], halo_s.at[2 * i + 1], halo_r.at[2 * i + 1], {"seq": left, "dp": d})
        return to_right, to_left

    cot_halo = halo(0, lambda half: c_hbm.at[:, pl.ds(half * HALF, HALF), :], c_halo)
    act_halo = halo(1, lambda half: a_v.at[half], a_halo)

    def start_halo(copies):
        @pl.when(s < 31)
        def _():
            copies[0].start()

        @pl.when(s > 0)
        def _():
            copies[1].start()

    def receive_halo(copies, dst):
        @pl.when(s > 0)
        def _():
            copies[0].wait_recv()

        @pl.when(s == 0)
        def _():
            dst[0] = jnp.zeros(dst.shape[1:], BF16)

        @pl.when(s < 31)
        def _():
            copies[1].wait_recv()

        @pl.when(s == 31)
        def _():
            dst[1] = jnp.zeros(dst.shape[1:], BF16)

    def sent_halo(copies):
        @pl.when(s < 31)
        def _():
            copies[0].wait_send()

        @pl.when(s > 0)
        def _():
            copies[1].wait_send()

    start_halo(cot_halo)

    loads[0].wait()
    loads[1].wait()

    def activate(i, carry):
        half = i // 24
        pair = lax.rem(i // 6, 4)
        lanes = pl.ds(pl.multiple_of(lax.rem(i, 6) * 128, 128), 128)
        v = f_v[half, pl.ds(pair * 2, 2), :, lanes].reshape(128, 128).astype(F32)
        sq = v * v
        t = jnp.tanh(ROOT * v * (1.0 + CUBIC * sq))
        cdf = 0.5 * (1.0 + t)
        act = v * cdf
        slope = cdf + 0.5 * v * (1.0 - t * t) * (ROOT * (1.0 + 3.0 * CUBIC * sq))
        a_v[half, pl.ds(pair * 2, 2), :, lanes] = act.astype(BF16).reshape(2, HALF, 128)
        rows = pl.ds(pl.multiple_of(pair * 128, 128), 128)
        d_v[half, rows, lanes] = slope
        at_v[half, lanes, rows] = act.T.astype(BF16)
        return carry

    lax.fori_loop(0, 48, activate, 0)

    def cols_of(j):
        return pl.ds(pl.multiple_of(j * TILE, TILE), TILE)

    def cots(ref, half, cols):
        return ref[half, :, :, cols].reshape(ROWS, TILE)

    def rows_of(ref, half):
        return ref[half].reshape(ROWS, WIDTH)

    def grad_terms(tap, terms, add):
        def body(j, carry):
            cols = cols_of(j)
            total = dot(at_v[terms[0][0]], cots(terms[0][1], terms[0][2], cols))
            for act_half, ref, half in terms[1:]:
                total = total + dot(at_v[act_half], cots(ref, half, cols))
            total = total.reshape(4, 4, 2, 24, TILE)
            if add:
                total = total + part[tap, :, :, :, :, cols]
            part[tap, :, :, :, :, cols] = total
            return carry

        lax.fori_loop(0, TILES, body, 0)

    core_copy = [
        remote(part.at[tap, :, :, 1 - core], mate_part.at[tap], core_s.at[tap], core_r.at[tap], {"seq": mate, "dp": d})
        for tap in range(3)
    ]
    y_copy = [
        [
            remote(ys.at[lax.rem(y + k, 4), tap], yr.at[k - 1, tap], y_s.at[tap, k - 1], y_r.at[tap, k - 1], y_partner(k))
            for k in range(1, 4)
        ]
        for tap in range(3)
    ]
    x_copy = [
        [
            remote(xs.at[lax.rem(x + k, 4), tap], xr.at[k - 1, tap], x_s.at[tap, k - 1], x_r.at[tap, k - 1], x_partner(k))
            for k in range(1, 4)
        ]
        for tap in range(3)
    ]
    z_copy = [
        [
            remote(zs.at[lax.rem(z + k, 8), tap], zr.at[k - 1, tap], z_s.at[tap, k - 1], z_r.at[tap, k - 1], z_partner(k))
            for k in range(1, 8)
        ]
        for tap in range(3)
    ]

    lane = lax.broadcasted_iota(jnp.int32, (48, 128), 1)
    lane96 = lax.broadcasted_iota(jnp.int32, (96, 128), 1)

    def send_y(tap):
        core_copy[tap].wait_recv()

        def body(i, carry):
            total = part[tap, :, i, core] + mate_part[tap, :, i]
            total = total.reshape(96, WIDTH)
            for to in range(4):
                full = total[:, FULL_TILE[to] * 128 : FULL_TILE[to] * 128 + 128]
                shared = total[:, SHARED_TILE[to] * 128 : SHARED_TILE[to] * 128 + 128]
                a, b = shared[:48], shared[48:]
                if to % 2 == 0:
                    packed = jnp.where(lane < 64, a, pltpu.roll(b, 64, 1))
                else:
                    packed = jnp.where(lane < 64, pltpu.roll(a, 64, 1), b)
                ys[to, tap, i, :96] = full.astype(BF16)
                ys[to, tap, i, 96:] = packed.astype(BF16)
            return carry

        lax.fori_loop(0, 4, body, 0)
        for copy in y_copy[tap]:
            copy.start()

    def send_x(tap):
        for copy in y_copy[tap]:
            copy.wait_recv()

        def body(i, carry):
            total = ys[y, tap, i].astype(F32)
            for k in range(3):
                total = total + yr[k, tap, i].astype(F32)
            xs[i, tap] = total.astype(BF16)
            return carry

        lax.fori_loop(0, 4, body, 0)
        for copy in x_copy[tap]:
            copy.start()

    def send_z(tap):
        for copy in x_copy[tap]:
            copy.wait_recv()
        total = xs[x, tap].astype(F32)
        for k in range(3):
            total = total + xr[k, tap].astype(F32)
        full, packed = total[:96], total[96:]
        rest = jnp.concatenate([packed, pltpu.roll(packed, 64, 1)], axis=0)
        odd = lax.rem(y, 2) == 1
        first = jnp.where(odd, jnp.where(lane96 < 64, rest, pltpu.roll(full, 64, 1)), full)
        second = jnp.where(odd, pltpu.roll(full, 96, 1), pltpu.roll(jnp.where(lane96 >= 96, full, rest), 32, 1))
        zs[0:4, tap] = first.reshape(4, 24, 128)
        zs[4:8, tap] = second.reshape(4, 24, 128)
        for copy in z_copy[tap]:
            copy.start()

    def conv_inner(j, carry):
        cols = cols_of(j)
        head, tail = rows_of(a_v, 0), rows_of(a_v, 1)
        conv[0, :, cols] = dot(head, k_v[1, :, cols]) + dot(tail, k_v[2, :, cols])
        conv[1, :, cols] = dot(head, k_v[0, :, cols]) + dot(tail, k_v[1, :, cols])
        return carry

    def back_inner(j, carry):
        cols = cols_of(j)
        head, tail = rows_of(c_v, 0), rows_of(c_v, 1)
        back[0, :, cols] = dot_t(tail, k_v[0, cols, :]) + dot_t(head, k_v[1, cols, :])
        back[1, :, cols] = dot_t(tail, k_v[1, cols, :]) + dot_t(head, k_v[2, cols, :])
        return carry

    def back_outer(j, carry):
        cols = cols_of(j)
        for half, tap in ((0, 2), (1, 0)):
            total = back[half, :, cols] + dot_t(rows_of(c_halo, half), k_v[tap, cols, :])
            own = c_v[half, :, :, cols].reshape(ROWS, TILE).astype(F32)
            result = own + d_v[half, :, cols] * total
            g_v[half, :, :, cols] = result.astype(BF16).reshape(SEQS, HALF, TILE)
        return carry

    def conv_outer(j, carry):
        cols = cols_of(j)
        for half, tap in ((0, 0), (1, 2)):
            total = conv[half, :, cols] + dot(rows_of(a_halo, half), k_v[tap, :, cols])
            own = f_v[half, :, :, cols].reshape(ROWS, TILE).astype(F32)
            o_v[half, :, :, cols] = (own + total).astype(BF16).reshape(SEQS, HALF, TILE)
        return carry

    loads[2].wait()
    loads[3].wait()
    grad_terms(1, [(0, c_v, 0), (1, c_v, 1)], False)
    core_copy[1].start()
    grad_terms(0, [(0, c_v, 1)], False)
    grad_terms(2, [(1, c_v, 0)], False)
    send_y(1)
    loads[4].wait()
    lax.fori_loop(0, TILES, back_inner, 0)
    receive_halo(cot_halo, c_halo)
    start_halo(act_halo)
    grad_terms(0, [(1, c_halo, 1)], True)
    core_copy[0].start()
    grad_terms(2, [(0, c_halo, 0)], True)
    core_copy[2].start()
    send_x(1)
    send_y(0)
    send_y(2)
    lax.fori_loop(0, TILES, conv_inner, 0)
    lax.fori_loop(0, TILES, back_outer, 0)
    stores = []
    for half in range(2):
        rows = pl.ds(half * HALF, HALF)
        stores.append(pltpu.make_async_copy(g_v.at[half], gin_hbm.at[:, rows, :], out_sem.at[half]))
    stores[0].start()
    stores[1].start()
    send_z(1)
    send_x(0)
    receive_halo(act_halo, a_halo)
    lax.fori_loop(0, TILES, conv_outer, 0)
    for half in range(2):
        rows = pl.ds(half * HALF, HALF)
        stores.append(pltpu.make_async_copy(o_v.at[half], out_hbm.at[:, rows, :], out_sem.at[2 + half]))
    stores[2].start()
    stores[3].start()
    send_z(0)
    send_x(2)
    send_z(2)
    for tap in (1, 0, 2):
        for copy in z_copy[tap]:
            copy.wait_recv()
        total = zs[z, tap]
        for k in range(7):
            total = total + zr[k, tap]
        wg_ref[tap] = (total * FACTOR)[:, :96]

    sent_halo(cot_halo)
    sent_halo(act_halo)
    for tap in range(3):
        core_copy[tap].wait_send()
        for copy in y_copy[tap] + x_copy[tap] + z_copy[tap]:
            copy.wait_send()
    for store in stores:
        store.wait()


def on_device(features, weights, cotangent):
    block = jax.ShapeDtypeStruct(features.shape, BF16)
    hbm = pl.BlockSpec(memory_space=pl.ANY)
    vmem = pltpu.VMEM
    dma = pltpu.SemaphoreType.DMA
    halves = (2, SEQS, HALF, WIDTH)
    return pl.pallas_call(
        kernel,
        out_shape=(block, block, jax.ShapeDtypeStruct((3, 24, 96), F32)),
        in_specs=[hbm, hbm, hbm],
        out_specs=(hbm, hbm, pl.BlockSpec(memory_space=pltpu.VMEM)),
        scratch_shapes=[
            vmem(halves, BF16),
            vmem(halves, BF16),
            vmem((3, WIDTH, WIDTH), BF16),
            vmem(halves, BF16),
            vmem((2, WIDTH, ROWS), BF16),
            vmem((2, ROWS, WIDTH), F32),
            vmem(halves, BF16),
            vmem(halves, BF16),
            vmem((2, ROWS, WIDTH), F32),
            vmem((2, ROWS, WIDTH), F32),
            vmem(halves, BF16),
            vmem(halves, BF16),
            vmem((3, 4, 4, 2, 24, WIDTH), F32),
            vmem((3, 4, 4, 24, WIDTH), F32),
            vmem((4, 3, 4, 144, 128), BF16),
            vmem((3, 3, 4, 144, 128), BF16),
            vmem((4, 3, 144, 128), BF16),
            vmem((3, 3, 144, 128), BF16),
            vmem((8, 3, 24, 128), F32),
            vmem((7, 3, 24, 128), F32),
            dma((5,)), dma((4,)), dma((4,)), dma((4,)), dma((3,)), dma((3,)),
            dma((3, 3)), dma((3, 3)), dma((3, 3)), dma((3, 3)), dma((3, 7)), dma((3, 7)),
        ],
        compiler_params=pltpu.CompilerParams(
            collective_id=0, has_side_effects=True, vmem_limit_bytes=58 * 1024 * 1024
        ),
        cost_estimate=pl.CostEstimate(
            flops=18 * 2 * ROWS * WIDTH * WIDTH, bytes_accessed=10 * 1024 * 1024, transcendentals=2 * ROWS * WIDTH
        ),
    )(features, weights, cotangent)


def solution(mesh):
    in_specs = (P("dp", "seq", None), P(), P("dp", "seq", None))
    out_specs = (P("dp", "seq", None), P("dp", "seq", None), P(None, "seq", "dp"))
    return jax.shard_map(
        on_device, mesh=mesh, in_specs=in_specs, out_specs=out_specs, check_vma=False
    )
```

```python
import functools
import math

import jax
import jax.numpy as jnp
from jax import lax
from jax.experimental import pallas as pl
from jax.experimental.pallas import tpu as pltpu
from jax.sharding import PartitionSpec as P

MESH = pl.DeviceIdType.MESH
BF16 = jnp.bfloat16
F32 = jnp.float32
SEQS = 8
HALF = 64
WIDTH = 768
ROWS = SEQS * HALF
TILE = 256
TILES = WIDTH // TILE
ROOT = math.sqrt(2.0 / math.pi)
CUBIC = 0.044715
FACTOR = 1.0 / math.sqrt(64 * 4096)
FULL_TILE = (0, 2, 3, 5)
SHARED_TILE = (1, 1, 4, 4)


def dot(a, b):
    return lax.dot_general(a, b, (((1,), (0,)), ((), ())), preferred_element_type=F32)


def dot_t(a, b):
    return lax.dot_general(a, b, (((1,), (1,)), ((), ())), preferred_element_type=F32)


def kernel(
    f_hbm, k_hbm, c_hbm, out_hbm, gin_hbm, wg_ref,
    f_v, c_v, k_v, a_v, at_v, d_v, c_halo, a_halo, conv, back, o_v, g_v,
    part, mate_part, ys, yr, xs, xr, zs, zr, xs2, xr2, ys2, yr2,
    in_sem, out_sem, halo_s, halo_r, core_s, core_r, y_s, y_r, x_s, x_r, z_s, z_r,
    y2_s, y2_r, x2_s, x2_r,
):
    s = lax.axis_index("seq")
    d = lax.axis_index("dp")
    core = lax.rem(s, 2)
    x = lax.rem(s // 2, 4)
    z_lo = s // 8
    y = d // 2
    z_hi = lax.rem(d, 2)
    z = z_hi * 4 + z_lo
    left = lax.rem(s + 31, 32)
    right = lax.rem(s + 1, 32)
    mate = s + 1 - 2 * core

    def y_partner(k):
        return {"seq": s, "dp": lax.rem(y + k, 4) * 2 + z_hi}

    def x_partner(k):
        return {"seq": (z_lo * 4 + lax.rem(x + k, 4)) * 2 + core, "dp": d}

    def z_partner(k):
        other = lax.rem(z + k, 8)
        return {"seq": (lax.rem(other, 4) * 4 + x) * 2 + core, "dp": y * 2 + other // 4}

    loads = []
    for half in range(2):
        rows = pl.ds(half * HALF, HALF)
        loads.append(pltpu.make_async_copy(f_hbm.at[:, rows, :], f_v.at[half], in_sem.at[half]))
    for half in range(2):
        rows = pl.ds(half * HALF, HALF)
        loads.append(pltpu.make_async_copy(c_hbm.at[:, rows, :], c_v.at[half], in_sem.at[2 + half]))
    loads.append(pltpu.make_async_copy(k_hbm, k_v, in_sem.at[4]))
    for load in loads:
        load.start()

    barrier = pltpu.get_barrier_semaphore()
    partners = [{"seq": left, "dp": d}, {"seq": right, "dp": d}]
    partners += [y_partner(k) for k in range(1, 4)]
    partners += [x_partner(k) for k in range(1, 4)]
    partners += [z_partner(k) for k in range(1, 8)]
    for partner in partners:
        pl.semaphore_signal(barrier, inc=1, device_id=partner, device_id_type=MESH)
    pl.semaphore_wait(barrier, len(partners))

    def remote(src, dst, send_sem, recv_sem, device):
        return pltpu.make_async_remote_copy(
            src_ref=src, dst_ref=dst, send_sem=send_sem, recv_sem=recv_sem,
            device_id=device, device_id_type=MESH,
        )

    def halo(i, src, dst):
        to_right = remote(src(1), dst.at[0], halo_s.at[2 * i], halo_r.at[2 * i], {"seq": right, "dp": d})
        to_left = remote(src(0), dst.at[1], halo_s.at[2 * i + 1], halo_r.at[2 * i + 1], {"seq": left, "dp": d})
        return to_right, to_left

    cot_halo = halo(0, lambda half: c_hbm.at[:, pl.ds(half * HALF, HALF), :], c_halo)
    act_halo = halo(1, lambda half: a_v.at[half], a_halo)

    def start_halo(copies):
        @pl.when(s < 31)
        def _():
            copies[0].start()

        @pl.when(s > 0)
        def _():
            copies[1].start()

    def receive_early(i, dst):
        slot = 1 - core
        remote(dst.at[0], dst.at[slot], halo_s.at[2 * i], halo_r.at[2 * i + slot], {"seq": mate, "dp": d}).wait_recv()

    def receive_late(i, dst):
        inside = jnp.logical_and(s > 0, s < 31)

        @pl.when(inside)
        def _():
            remote(dst.at[0], dst.at[core], halo_s.at[2 * i], halo_r.at[2 * i + core], {"seq": mate, "dp": d}).wait_recv()

        @pl.when(jnp.logical_not(inside))
        def _():
            dst[core] = jnp.zeros(dst.shape[1:], BF16)

    def sent_halo(copies):
        @pl.when(s < 31)
        def _():
            copies[0].wait_send()

        @pl.when(s > 0)
        def _():
            copies[1].wait_send()

    start_halo(cot_halo)

    loads[0].wait()
    loads[1].wait()

    def activate(i, carry):
        half = i // 24
        pair = lax.rem(i // 6, 4)
        lanes = pl.ds(pl.multiple_of(lax.rem(i, 6) * 128, 128), 128)
        v = f_v[half, pl.ds(pair * 2, 2), :, lanes].reshape(128, 128).astype(F32)
        t = jnp.tanh(ROOT * v * (1.0 + CUBIC * (v * v)))
        act = v * (0.5 * (1.0 + t))
        a_v[half, pl.ds(pair * 2, 2), :, lanes] = act.astype(BF16).reshape(2, HALF, 128)
        rows = pl.ds(pl.multiple_of(pair * 128, 128), 128)
        at_v[half, lanes, rows] = act.T.astype(BF16)
        return carry

    lax.fori_loop(0, 48, activate, 0, unroll=2)

    def derive(i, carry):
        half = i // 24
        pair = lax.rem(i // 6, 4)
        lanes = pl.ds(pl.multiple_of(lax.rem(i, 6) * 128, 128), 128)
        v = f_v[half, pl.ds(pair * 2, 2), :, lanes].reshape(128, 128).astype(F32)
        sq = v * v
        t = jnp.tanh(ROOT * v * (1.0 + CUBIC * sq))
        slope = 0.5 * (1.0 + t) + 0.5 * v * (1.0 - t * t) * (ROOT * (1.0 + 3.0 * CUBIC * sq))
        d_v[half, pl.ds(pl.multiple_of(pair * 128, 128), 128), lanes] = slope
        return carry

    def cols_of(j):
        return pl.ds(pl.multiple_of(j * TILE, TILE), TILE)

    def cots(ref, half, cols):
        return ref[half, :, :, cols].reshape(ROWS, TILE)

    def rows_of(ref, half):
        return ref[half].reshape(ROWS, WIDTH)

    def core_copy(tap, j):
        return remote(
            part.at[tap, j, :, :, 1 - core], mate_part.at[tap, j], core_s.at[tap, j], core_r.at[tap, j],
            {"seq": mate, "dp": d},
        )

    def grad_terms(tap, terms, add, send):
        def body(j, carry):
            cols = cols_of(j)
            total = dot(at_v[terms[0][0]], cots(terms[0][1], terms[0][2], cols))
            for act_half, ref, half in terms[1:]:
                total = total + dot(at_v[act_half], cots(ref, half, cols))
            total = total.reshape(4, 4, 2, 24, TILE)
            if add:
                total = total + part[tap, j]
            part[tap, j] = total
            if send:
                core_copy(tap, j).start()
            return carry

        lax.fori_loop(0, TILES, body, 0)

    def y_copy(tap):
        return [
        remote(ys.at[lax.rem(y + k, 4), tap], yr.at[k - 1, tap], y_s.at[tap, k - 1], y_r.at[tap, k - 1], y_partner(k))
        for k in range(1, 4)
        ]

    def x_copy(tap):
        return [
        remote(xs.at[lax.rem(x + k, 4), tap], xr.at[k - 1, tap], x_s.at[tap, k - 1], x_r.at[tap, k - 1], x_partner(k))
        for k in range(1, 4)
        ]

    def z_copy(tap):
        return [
        remote(zs.at[lax.rem(z + k, 8), tap], zr.at[k - 1, tap], z_s.at[tap, k - 1], z_r.at[tap, k - 1], z_partner(k))
        for k in range(1, 8)
        ]


    def x_first(tap):
        return [
            remote(xs2.at[lax.rem(x + k, 4), tap], xr2.at[k - 1, tap], x2_s.at[tap, k - 1], x2_r.at[tap, k - 1], x_partner(k))
            for k in range(1, 4)
        ]

    def y_second(tap):
        return [
        remote(ys2.at[lax.rem(y + k, 4), tap], yr2.at[k - 1, tap], y2_s.at[tap, k - 1], y2_r.at[tap, k - 1], y_partner(k))
        for k in range(1, 4)
        ]

    lane16 = lax.broadcasted_iota(jnp.int32, (16, 128), 1)
    lane32 = lax.broadcasted_iota(jnp.int32, (32, 128), 1)
    lane96 = lax.broadcasted_iota(jnp.int32, (96, 128), 1)

    def columns_for(to, tiles, lane):
        full = tiles[FULL_TILE[to]]
        shared = tiles[SHARED_TILE[to]]
        a, b = shared[: lane.shape[0]], shared[lane.shape[0] :]
        if to % 2 == 0:
            return full, jnp.where(lane < 64, a, pltpu.roll(b, 64, 1))
        return full, jnp.where(lane < 64, pltpu.roll(a, 64, 1), b)

    def receive_core(tap):
        for j in range(TILES):
            core_copy(tap, j).wait_recv()

    def send_y(tap):
        def body(i, carry):
            tiles = []
            for j in range(TILES):
                total = part[tap, j, :, i, core, :16] + mate_part[tap, j, :, i, :16]
                total = total.reshape(64, TILE)
                tiles += [total[:, :128], total[:, 128:]]
            for to in range(4):
                full, packed = columns_for(to, tiles, lane32)
                ys[to, tap, i, :64] = full.astype(BF16)
                ys[to, tap, i, 64:] = packed.astype(BF16)
            return carry

        lax.fori_loop(0, 4, body, 0)
        for copy in y_copy(tap):
            copy.start()

    def send_x_first(tap):
        def body(i, carry):
            for j in range(TILES):
                total = part[tap, j, :, i, core, 16:] + mate_part[tap, j, :, i, 16:]
                xs2[i, tap, :, j * TILE : (j + 1) * TILE] = total.reshape(32, TILE).astype(BF16)
            return carry

        lax.fori_loop(0, 4, body, 0)
        for copy in x_first(tap):
            copy.start()

    def send_y_second(tap):
        for copy in x_first(tap):
            copy.wait_recv()
        tiles = []
        for j in range(6):
            cols = slice(j * 128, j * 128 + 128)
            total = xs2[x, tap, :, cols].astype(F32)
            for k in range(3):
                total = total + xr2[k, tap, :, cols].astype(F32)
            tiles.append(total)
        for to in range(4):
            full, packed = columns_for(to, tiles, lane16)
            ys2[to, tap, :32] = full.astype(BF16)
            ys2[to, tap, 32:] = packed.astype(BF16)
        for copy in y_second(tap):
            copy.start()

    def send_first(tap):
        receive_core(tap)
        send_y(tap)
        send_x_first(tap)

    def send_x(tap):
        for copy in y_copy(tap):
            copy.wait_recv()

        def body(i, carry):
            total = ys[y, tap, i].astype(F32)
            for k in range(3):
                total = total + yr[k, tap, i].astype(F32)
            xs[i, tap] = total.astype(BF16)
            return carry

        lax.fori_loop(0, 4, body, 0)
        for copy in x_copy(tap):
            copy.start()

    def send_z(tap):
        for copy in x_copy(tap) + y_second(tap):
            copy.wait_recv()

        def gathered(own, others, rows):
            total = own.astype(F32)
            for k in range(3):
                total = total + others[k, tap].astype(F32)
            packed = total[4 * rows :]
            rest = jnp.concatenate([packed, pltpu.roll(packed, 64, 1)], axis=0)
            return total[: 4 * rows].reshape(4, rows, 128), rest.reshape(4, rows, 128)

        full_a, rest_a = gathered(xs[x, tap], xr, 16)
        full_b, rest_b = gathered(ys2[y, tap], yr2, 8)
        full = jnp.concatenate([full_a, full_b], axis=1).reshape(96, 128)
        rest = jnp.concatenate([rest_a, rest_b], axis=1).reshape(96, 128)
        odd = lax.rem(y, 2) == 1
        first = jnp.where(odd, jnp.where(lane96 < 64, rest, pltpu.roll(full, 64, 1)), full)
        second = jnp.where(odd, pltpu.roll(full, 96, 1), pltpu.roll(jnp.where(lane96 >= 96, full, rest), 32, 1))
        zs[0:4, tap] = first.reshape(4, 24, 128)
        zs[4:8, tap] = second.reshape(4, 24, 128)
        for copy in z_copy(tap):
            copy.start()

    def conv_inner(j, carry):
        cols = cols_of(j)
        head, tail = rows_of(a_v, 0), rows_of(a_v, 1)
        conv[0, :, cols] = dot(head, k_v[1, :, cols]) + dot(tail, k_v[2, :, cols])
        conv[1, :, cols] = dot(head, k_v[0, :, cols]) + dot(tail, k_v[1, :, cols])
        return carry

    def back_inner(j, carry):
        cols = cols_of(j)
        head, tail = rows_of(c_v, 0), rows_of(c_v, 1)
        back[0, :, cols] = dot_t(tail, k_v[0, cols, :]) + dot_t(head, k_v[1, cols, :])
        back[1, :, cols] = dot_t(tail, k_v[1, cols, :]) + dot_t(head, k_v[2, cols, :])
        return carry

    def back_outer(j, carry):
        cols = cols_of(j)
        for half, tap in ((0, 2), (1, 0)):
            total = back[half, :, cols] + dot_t(rows_of(c_halo, half), k_v[tap, cols, :])
            own = c_v[half, :, :, cols].reshape(ROWS, TILE).astype(F32)
            result = own + d_v[half, :, cols] * total
            g_v[half, :, :, cols] = result.astype(BF16).reshape(SEQS, HALF, TILE)
        return carry

    def conv_outer(j, carry):
        cols = cols_of(j)
        for half, tap in ((0, 0), (1, 2)):
            total = conv[half, :, cols] + dot(rows_of(a_halo, half), k_v[tap, :, cols])
            own = f_v[half, :, :, cols].reshape(ROWS, TILE).astype(F32)
            o_v[half, :, :, cols] = (own + total).astype(BF16).reshape(SEQS, HALF, TILE)
        return carry

    stores = []

    def store(i, source, target):
        for half in range(2):
            rows = pl.ds(half * HALF, HALF)
            stores.append(pltpu.make_async_copy(source.at[half], target.at[:, rows, :], out_sem.at[2 * i + half]))
            stores[-1].start()

    early, late = 2 * core, 2 - 2 * core

    def grad_outer(tap, half):
        grad_terms(tap, [(half, c_halo, half)], True, True)

    loads[2].wait()
    loads[3].wait()
    grad_terms(1, [(0, c_v, 0), (1, c_v, 1)], False, True)
    grad_terms(0, [(0, c_v, 1)], False, False)
    send_first(1)
    grad_terms(2, [(1, c_v, 0)], False, False)
    receive_early(0, c_halo)
    grad_outer(early, 1 - core)
    loads[4].wait()
    lax.fori_loop(0, 1, back_inner, 0)
    receive_late(0, c_halo)
    grad_outer(late, core)
    send_first(late)
    send_first(early)
    start_halo(act_halo)
    send_x(1)
    send_y_second(1)
    lax.fori_loop(1, TILES, back_inner, 0)
    lax.fori_loop(0, 48, derive, 0, unroll=2)
    send_z(1)
    send_x(late)
    send_y_second(late)
    lax.fori_loop(0, TILES, back_outer, 0)
    store(0, g_v, gin_hbm)
    send_x(early)
    send_y_second(early)
    lax.fori_loop(0, 2, conv_inner, 0)
    send_z(late)
    send_z(early)
    lax.fori_loop(2, TILES, conv_inner, 0)
    receive_early(1, a_halo)
    receive_late(1, a_halo)
    lax.fori_loop(0, TILES, conv_outer, 0)
    store(1, o_v, out_hbm)
    for tap in (1, late, early):
        for copy in z_copy(tap):
            copy.wait_recv()
        total = zs[z, tap]
        for k in range(7):
            total = total + zr[k, tap]
        wg_ref[tap] = (total * FACTOR)[:, :96]

    sent_halo(cot_halo)
    sent_halo(act_halo)
    for tap in range(3):
        for j in range(TILES):
            core_copy(tap, j).wait_send()
        for copy in y_copy(tap) + x_copy(tap) + z_copy(tap) + x_first(tap) + y_second(tap):
            copy.wait_send()
    for pending in stores:
        pending.wait()


def on_device(features, weights, cotangent):
    block = jax.ShapeDtypeStruct(features.shape, BF16)
    hbm = pl.BlockSpec(memory_space=pl.ANY)
    vmem = pltpu.VMEM
    dma = pltpu.SemaphoreType.DMA
    halves = (2, SEQS, HALF, WIDTH)
    return pl.pallas_call(
        kernel,
        out_shape=(block, block, jax.ShapeDtypeStruct((3, 24, 96), F32)),
        in_specs=[hbm, hbm, hbm],
        out_specs=(hbm, hbm, pl.BlockSpec(memory_space=pltpu.VMEM)),
        scratch_shapes=[
            vmem(halves, BF16),
            vmem(halves, BF16),
            vmem((3, WIDTH, WIDTH), BF16),
            vmem(halves, BF16),
            vmem((2, WIDTH, ROWS), BF16),
            vmem((2, ROWS, WIDTH), F32),
            vmem(halves, BF16),
            vmem(halves, BF16),
            vmem((2, ROWS, WIDTH), F32),
            vmem((2, ROWS, WIDTH), F32),
            vmem(halves, BF16),
            vmem(halves, BF16),
            vmem((3, TILES, 4, 4, 2, 24, TILE), F32),
            vmem((3, TILES, 4, 4, 24, TILE), F32),
            vmem((4, 3, 4, 96, 128), BF16),
            vmem((3, 3, 4, 96, 128), BF16),
            vmem((4, 3, 96, 128), BF16),
            vmem((3, 3, 96, 128), BF16),
            vmem((8, 3, 24, 128), F32),
            vmem((7, 3, 24, 128), F32),
            vmem((4, 3, 32, WIDTH), BF16),
            vmem((3, 3, 32, WIDTH), BF16),
            vmem((4, 3, 48, 128), BF16),
            vmem((3, 3, 48, 128), BF16),
            dma((5,)), dma((4,)), dma((4,)), dma((4,)), dma((3, 3)), dma((3, 3)),
            dma((3, 3)), dma((3, 3)), dma((3, 3)), dma((3, 3)), dma((3, 7)), dma((3, 7)),
            dma((3, 3)), dma((3, 3)), dma((3, 3)), dma((3, 3)),
        ],
        compiler_params=pltpu.CompilerParams(
            collective_id=0, has_side_effects=True, vmem_limit_bytes=50 * 1024 * 1024
        ),
        cost_estimate=pl.CostEstimate(
            flops=18 * 2 * ROWS * WIDTH * WIDTH, bytes_accessed=10 * 1024 * 1024, transcendentals=2 * ROWS * WIDTH
        ),
    )(features, weights, cotangent)


def solution(mesh):
    in_specs = (P("dp", "seq", None), P(), P("dp", "seq", None))
    out_specs = (P("dp", "seq", None), P("dp", "seq", None), P(None, "seq", "dp"))
    return jax.shard_map(
        on_device, mesh=mesh, in_specs=in_specs, out_specs=out_specs, check_vma=False
    )
```

```python
import functools
import math

import jax
import jax.numpy as jnp
from jax import lax
from jax.experimental import pallas as pl
from jax.experimental.pallas import tpu as pltpu
from jax.sharding import PartitionSpec as P

MESH = pl.DeviceIdType.MESH
BF16 = jnp.bfloat16
F32 = jnp.float32
SEQS = 8
HALF = 64
WIDTH = 768
ROWS = SEQS * HALF
TILE = 256
TILES = WIDTH // TILE
ROOT = math.sqrt(2.0 / math.pi)
CUBIC = 0.044715
FACTOR = 1.0 / math.sqrt(64 * 4096)
PAIRS = ((0, 2), (3, 5), (1, 4))
CHUNKS = ((0, 1), (2,))
SLICES = (((0, 128), (256, 256), (640, 128)), ((128, 128), (512, 128)))
PIECES = ((0, 5), (5, 3))


def dot(a, b):
    return lax.dot_general(a, b, (((1,), (0,)), ((), ())), preferred_element_type=F32)


def dot_t(a, b):
    return lax.dot_general(a, b, (((1,), (1,)), ((), ())), preferred_element_type=F32)


def kernel(
    f_hbm, k_hbm, c_hbm, out_hbm, gin_hbm, wg_ref,
    f_v, c_v, k_v, a_v, at_v, d_v, c_halo, a_halo, conv, back, o_v, g_v,
    part, mate_part, ys, yr, xs, xr, zs, zr, xs2, xr2, ys2, yr2,
    in_sem, out_sem, halo_s, halo_r, core_s, core_r, y_s, y_r, x_s, x_r, z_s, z_r,
    y2_s, y2_r, x2_s, x2_r,
):
    s = lax.axis_index("seq")
    d = lax.axis_index("dp")
    core = lax.rem(s, 2)
    x = lax.rem(s // 2, 4)
    z_lo = s // 8
    y = d // 2
    z_hi = lax.rem(d, 2)
    z = z_hi * 4 + z_lo
    left = lax.rem(s + 31, 32)
    right = lax.rem(s + 1, 32)
    mate = s + 1 - 2 * core

    def y_partner(k):
        return {"seq": s, "dp": lax.rem(y + k, 4) * 2 + z_hi}

    def x_partner(k):
        return {"seq": (z_lo * 4 + lax.rem(x + k, 4)) * 2 + core, "dp": d}

    def z_partner(k):
        other = lax.rem(z + k, 8)
        return {"seq": (lax.rem(other, 4) * 4 + x) * 2 + core, "dp": y * 2 + other // 4}

    loads = []
    for half in range(2):
        rows = pl.ds(half * HALF, HALF)
        loads.append(pltpu.make_async_copy(f_hbm.at[:, rows, :], f_v.at[half], in_sem.at[half]))
    for half in range(2):
        rows = pl.ds(half * HALF, HALF)
        loads.append(pltpu.make_async_copy(c_hbm.at[:, rows, :], c_v.at[half], in_sem.at[2 + half]))
    loads.append(pltpu.make_async_copy(k_hbm, k_v, in_sem.at[4]))
    for load in loads:
        load.start()

    barrier = pltpu.get_barrier_semaphore()
    partners = [{"seq": left, "dp": d}, {"seq": right, "dp": d}]
    partners += [y_partner(k) for k in range(1, 4)]
    partners += [x_partner(k) for k in range(1, 4)]
    partners += [z_partner(k) for k in range(1, 8)]
    for partner in partners:
        pl.semaphore_signal(barrier, inc=1, device_id=partner, device_id_type=MESH)
    pl.semaphore_wait(barrier, len(partners))

    def remote(src, dst, send_sem, recv_sem, device):
        return pltpu.make_async_remote_copy(
            src_ref=src, dst_ref=dst, send_sem=send_sem, recv_sem=recv_sem,
            device_id=device, device_id_type=MESH,
        )

    def halo(i, src, dst, where):
        to_right = remote(src(1), dst.at[(0, *where)], halo_s.at[2 * i], halo_r.at[2 * i], {"seq": right, "dp": d})
        to_left = remote(src(0), dst.at[(1, *where)], halo_s.at[2 * i + 1], halo_r.at[2 * i + 1], {"seq": left, "dp": d})
        return to_right, to_left

    every = slice(None)
    cot_parts, act_parts = [], []
    for chunk in SLICES:
        cot_parts.append([(len(cot_parts) * 3 + i, (every, every, pl.ds(*cols))) for i, cols in enumerate(chunk)])
    for i, piece in enumerate(PIECES):
        act_parts.append([(5 + i, (pl.ds(*piece),))])
    cot_halo = [[halo(i, lambda half, p=p: c_v.at[(half, *p)], c_halo, p) for i, p in chunk] for chunk in cot_parts]
    act_halo = [[halo(i, lambda half, p=p: a_v.at[(half, *p)], a_halo, p) for i, p in chunk] for chunk in act_parts]

    def start_halo(chunk):
        @pl.when(s < 31)
        def _():
            for copies in chunk:
                copies[0].start()

        @pl.when(s > 0)
        def _():
            for copies in chunk:
                copies[1].start()

    def halo_into(i, dst, slot, where):
        return remote(
            dst.at[(0, *where)], dst.at[(slot, *where)], halo_s.at[2 * i], halo_r.at[2 * i + slot], {"seq": mate, "dp": d}
        )

    def receive_early(dst, parts):
        for i, where in parts:
            halo_into(i, dst, 1 - core, where).wait_recv()

    def receive_late(dst, parts):
        inside = jnp.logical_and(s > 0, s < 31)

        @pl.when(inside)
        def _():
            for i, where in parts:
                halo_into(i, dst, core, where).wait_recv()

        @pl.when(jnp.logical_not(inside))
        def _():
            for _, where in parts:
                blank = dst.at[(core, *where)]
                blank[...] = jnp.zeros(blank.shape, BF16)

    def sent_halo(copies):
        @pl.when(s < 31)
        def _():
            copies[0].wait_send()

        @pl.when(s > 0)
        def _():
            copies[1].wait_send()

    loads[2].wait()
    loads[3].wait()
    for chunk in cot_halo:
        start_halo(chunk)

    loads[0].wait()
    loads[1].wait()

    def activate(i, carry):
        half = i // 24
        pair = lax.rem(i // 6, 4)
        lanes = pl.ds(pl.multiple_of(lax.rem(i, 6) * 128, 128), 128)
        v = f_v[half, pl.ds(pair * 2, 2), :, lanes].reshape(128, 128).astype(F32)
        t = jnp.tanh(ROOT * v * (1.0 + CUBIC * (v * v)))
        act = v * (0.5 * (1.0 + t))
        a_v[half, pl.ds(pair * 2, 2), :, lanes] = act.astype(BF16).reshape(2, HALF, 128)
        rows = pl.ds(pl.multiple_of(pair * 128, 128), 128)
        at_v[half, lanes, rows] = act.T.astype(BF16)
        return carry

    lax.fori_loop(0, 48, activate, 0, unroll=2)

    def derive(i, carry):
        half = i // 24
        pair = lax.rem(i // 6, 4)
        lanes = pl.ds(pl.multiple_of(lax.rem(i, 6) * 128, 128), 128)
        v = f_v[half, pl.ds(pair * 2, 2), :, lanes].reshape(128, 128).astype(F32)
        sq = v * v
        t = jnp.tanh(ROOT * v * (1.0 + CUBIC * sq))
        slope = 0.5 * (1.0 + t) + 0.5 * v * (1.0 - t * t) * (ROOT * (1.0 + 3.0 * CUBIC * sq))
        d_v[half, pl.ds(pl.multiple_of(pair * 128, 128), 128), lanes] = slope
        return carry

    def cols_of(j):
        return pl.ds(pl.multiple_of(j * TILE, TILE), TILE)

    def cots(ref, half, j):
        tiles = [ref[half, :, :, t * 128 : t * 128 + 128].reshape(ROWS, 128) for t in PAIRS[j]]
        return jnp.concatenate(tiles, axis=1)

    def rows_of(ref, half):
        return ref[half].reshape(ROWS, WIDTH)

    def core_copy(tap, j):
        return remote(
            part.at[tap, j, :, :, 1 - core], mate_part.at[tap, j], core_s.at[tap, j], core_r.at[tap, j],
            {"seq": mate, "dp": d},
        )

    def grad_terms(tap, terms, add, send, tiles=range(TILES)):
        for j in tiles:
            total = dot(at_v[terms[0][0]], cots(terms[0][1], terms[0][2], j))
            for act_half, ref, half in terms[1:]:
                total = total + dot(at_v[act_half], cots(ref, half, j))
            total = total.reshape(4, 4, 2, 24, TILE)
            if add:
                total = total + part[tap, j]
            part[tap, j] = total
            if send:
                core_copy(tap, j).start()

    def y_copy(tap, chunk):
        rows = pl.ds(64 * chunk, 64 - 32 * chunk)
        return [
            remote(
                ys.at[lax.rem(y + k, 4), tap, :, rows], yr.at[k - 1, tap, :, rows],
                y_s.at[tap, chunk, k - 1], y_r.at[tap, chunk, k - 1], y_partner(k),
            )
            for k in range(1, 4)
        ]

    def x_copy(tap):
        return [
        remote(xs.at[lax.rem(x + k, 4), tap], xr.at[k - 1, tap], x_s.at[tap, k - 1], x_r.at[tap, k - 1], x_partner(k))
        for k in range(1, 4)
        ]

    def z_copy(tap):
        return [
        remote(zs.at[lax.rem(z + k, 8), tap], zr.at[k - 1, tap], z_s.at[tap, k - 1], z_r.at[tap, k - 1], z_partner(k))
        for k in range(1, 8)
        ]


    def x_first(tap, chunk):
        cols = pl.ds(512 * chunk, 512 - 256 * chunk)
        return [
            remote(
                xs2.at[lax.rem(x + k, 4), tap, :, cols], xr2.at[k - 1, tap, :, cols],
                x2_s.at[tap, chunk, k - 1], x2_r.at[tap, chunk, k - 1], x_partner(k),
            )
            for k in range(1, 4)
        ]

    def y_second(tap):
        return [
        remote(ys2.at[lax.rem(y + k, 4), tap], yr2.at[k - 1, tap], y2_s.at[tap, k - 1], y2_r.at[tap, k - 1], y_partner(k))
        for k in range(1, 4)
        ]

    lane16 = lax.broadcasted_iota(jnp.int32, (16, 128), 1)
    lane32 = lax.broadcasted_iota(jnp.int32, (32, 128), 1)
    lane96 = lax.broadcasted_iota(jnp.int32, (96, 128), 1)

    def packed_for(to, shared, lane):
        a, b = shared[: lane.shape[0]], shared[lane.shape[0] :]
        if to % 2 == 0:
            return jnp.where(lane < 64, a, pltpu.roll(b, 64, 1))
        return jnp.where(lane < 64, pltpu.roll(a, 64, 1), b)

    def send_y(tap, chunk):
        def body(i, carry):
            for j in CHUNKS[chunk]:
                total = part[tap, j, :, i, core, :16] + mate_part[tap, j, :, i, :16]
                total = total.reshape(64, TILE)
                tiles = total[:, :128], total[:, 128:]
                if chunk == 0:
                    for half in range(2):
                        ys[2 * j + half, tap, i, :64] = tiles[half].astype(BF16)
                else:
                    for to in range(4):
                        ys[to, tap, i, 64:] = packed_for(to, tiles[to // 2], lane32).astype(BF16)
            return carry

        lax.fori_loop(0, 4, body, 0)
        for copy in y_copy(tap, chunk):
            copy.start()

    def send_x_first(tap, chunk):
        def body(i, carry):
            for j in CHUNKS[chunk]:
                total = part[tap, j, :, i, core, 16:] + mate_part[tap, j, :, i, 16:]
                xs2[i, tap, :, j * TILE : (j + 1) * TILE] = total.reshape(32, TILE).astype(BF16)
            return carry

        lax.fori_loop(0, 4, body, 0)
        for copy in x_first(tap, chunk):
            copy.start()

    def send_y_second(tap):
        for copy in x_first(tap, 0) + x_first(tap, 1):
            copy.wait_recv()
        tiles = []
        for j in range(6):
            cols = slice(j * 128, j * 128 + 128)
            total = xs2[x, tap, :, cols].astype(F32)
            for k in range(3):
                total = total + xr2[k, tap, :, cols].astype(F32)
            tiles.append(total)
        for to in range(4):
            ys2[to, tap, :32] = tiles[to].astype(BF16)
            ys2[to, tap, 32:] = packed_for(to, tiles[4 + to // 2], lane16).astype(BF16)
        for copy in y_second(tap):
            copy.start()

    def send_first(tap, chunk):
        for j in CHUNKS[chunk]:
            core_copy(tap, j).wait_recv()
        send_y(tap, chunk)
        send_x_first(tap, chunk)

    def send_x(tap):
        for copy in y_copy(tap, 0) + y_copy(tap, 1):
            copy.wait_recv()

        def body(i, carry):
            total = ys[y, tap, i].astype(F32)
            for k in range(3):
                total = total + yr[k, tap, i].astype(F32)
            xs[i, tap] = total.astype(BF16)
            return carry

        lax.fori_loop(0, 4, body, 0)
        for copy in x_copy(tap):
            copy.start()

    def send_z(tap):
        for copy in x_copy(tap) + y_second(tap):
            copy.wait_recv()

        def gathered(own, others, rows):
            total = own.astype(F32)
            for k in range(3):
                total = total + others[k, tap].astype(F32)
            packed = total[4 * rows :]
            rest = jnp.concatenate([packed, pltpu.roll(packed, 64, 1)], axis=0)
            return total[: 4 * rows].reshape(4, rows, 128), rest.reshape(4, rows, 128)

        full_a, rest_a = gathered(xs[x, tap], xr, 16)
        full_b, rest_b = gathered(ys2[y, tap], yr2, 8)
        full = jnp.concatenate([full_a, full_b], axis=1).reshape(96, 128)
        rest = jnp.concatenate([rest_a, rest_b], axis=1).reshape(96, 128)
        odd = lax.rem(y, 2) == 1
        first = jnp.where(odd, jnp.where(lane96 < 64, rest, pltpu.roll(full, 64, 1)), full)
        second = jnp.where(odd, pltpu.roll(full, 96, 1), pltpu.roll(jnp.where(lane96 >= 96, full, rest), 32, 1))
        zs[0:4, tap] = first.reshape(4, 24, 128)
        zs[4:8, tap] = second.reshape(4, 24, 128)
        for copy in z_copy(tap):
            copy.start()

    def conv_inner(j, carry):
        cols = cols_of(j)
        head, tail = rows_of(a_v, 0), rows_of(a_v, 1)
        conv[0, :, cols] = dot(head, k_v[1, :, cols]) + dot(tail, k_v[2, :, cols])
        conv[1, :, cols] = dot(head, k_v[0, :, cols]) + dot(tail, k_v[1, :, cols])
        return carry

    def back_inner(j, carry):
        cols = cols_of(j)
        head, tail = rows_of(c_v, 0), rows_of(c_v, 1)
        back[0, :, cols] = dot_t(tail, k_v[0, cols, :]) + dot_t(head, k_v[1, cols, :])
        back[1, :, cols] = dot_t(tail, k_v[1, cols, :]) + dot_t(head, k_v[2, cols, :])
        return carry

    def back_outer(j, carry):
        cols = cols_of(j)
        for half, tap in ((0, 2), (1, 0)):
            total = back[half, :, cols] + dot_t(rows_of(c_halo, half), k_v[tap, cols, :])
            own = c_v[half, :, :, cols].reshape(ROWS, TILE).astype(F32)
            result = own + d_v[half, :, cols] * total
            g_v[half, :, :, cols] = result.astype(BF16).reshape(SEQS, HALF, TILE)
        return carry

    def conv_outer(j, carry):
        cols = cols_of(j)
        for half, tap in ((0, 0), (1, 2)):
            total = conv[half, :, cols] + dot(rows_of(a_halo, half), k_v[tap, :, cols])
            own = f_v[half, :, :, cols].reshape(ROWS, TILE).astype(F32)
            o_v[half, :, :, cols] = (own + total).astype(BF16).reshape(SEQS, HALF, TILE)
        return carry

    stores = []

    def store(i, source, target):
        for half in range(2):
            rows = pl.ds(half * HALF, HALF)
            stores.append(pltpu.make_async_copy(source.at[half], target.at[:, rows, :], out_sem.at[2 * i + half]))
            stores[-1].start()

    early, late = 2 * core, 2 - 2 * core

    def grad_outer(tap, half, chunk):
        grad_terms(tap, [(half, c_halo, half)], True, True, CHUNKS[chunk])

    grad_terms(1, [(0, c_v, 0), (1, c_v, 1)], False, True)
    grad_terms(0, [(0, c_v, 1)], False, False)
    grad_terms(2, [(1, c_v, 0)], False, False)
    send_first(1, 0)
    send_first(1, 1)
    for chunk in range(2):
        receive_early(c_halo, cot_parts[chunk])
        grad_outer(early, 1 - core, chunk)
    loads[4].wait()
    for chunk in range(2):
        receive_late(c_halo, cot_parts[chunk])
        if chunk == 1:
            start_halo(act_halo[0])
        grad_outer(late, core, chunk)
        send_first(late, chunk)
        send_first(early, chunk)
    send_x(1)
    send_y_second(1)
    lax.fori_loop(0, TILES, back_inner, 0)
    lax.fori_loop(0, 48, derive, 0, unroll=2)
    send_x(late)
    send_y_second(late)
    send_x(early)
    send_y_second(early)
    start_halo(act_halo[1])
    send_z(1)
    lax.fori_loop(0, TILES, back_outer, 0)
    store(0, g_v, gin_hbm)
    send_z(late)
    send_z(early)
    lax.fori_loop(0, TILES, conv_inner, 0)
    for parts in act_parts:
        receive_early(a_halo, parts)
        receive_late(a_halo, parts)
    lax.fori_loop(0, TILES, conv_outer, 0)
    store(1, o_v, out_hbm)
    for tap in (1, late, early):
        for copy in z_copy(tap):
            copy.wait_recv()
        total = zs[z, tap]
        for k in range(7):
            total = total + zr[k, tap]
        wg_ref[tap] = (total * FACTOR)[:, :96]

    for chunk in cot_halo + act_halo:
        for copies in chunk:
            sent_halo(copies)
    for tap in range(3):
        for j in range(TILES):
            core_copy(tap, j).wait_send()
        for copy in y_copy(tap, 0) + y_copy(tap, 1) + x_first(tap, 0) + x_first(tap, 1):
            copy.wait_send()
        for copy in x_copy(tap) + z_copy(tap) + y_second(tap):
            copy.wait_send()
    for pending in stores:
        pending.wait()


def on_device(features, weights, cotangent):
    block = jax.ShapeDtypeStruct(features.shape, BF16)
    hbm = pl.BlockSpec(memory_space=pl.ANY)
    vmem = pltpu.VMEM
    dma = pltpu.SemaphoreType.DMA
    halves = (2, SEQS, HALF, WIDTH)
    return pl.pallas_call(
        kernel,
        out_shape=(block, block, jax.ShapeDtypeStruct((3, 24, 96), F32)),
        in_specs=[hbm, hbm, hbm],
        out_specs=(hbm, hbm, pl.BlockSpec(memory_space=pltpu.VMEM)),
        scratch_shapes=[
            vmem(halves, BF16),
            vmem(halves, BF16),
            vmem((3, WIDTH, WIDTH), BF16),
            vmem(halves, BF16),
            vmem((2, WIDTH, ROWS), BF16),
            vmem((2, ROWS, WIDTH), F32),
            vmem(halves, BF16),
            vmem(halves, BF16),
            vmem((2, ROWS, WIDTH), F32),
            vmem((2, ROWS, WIDTH), F32),
            vmem(halves, BF16),
            vmem(halves, BF16),
            vmem((3, TILES, 4, 4, 2, 24, TILE), F32),
            vmem((3, TILES, 4, 4, 24, TILE), F32),
            vmem((4, 3, 4, 96, 128), BF16),
            vmem((3, 3, 4, 96, 128), BF16),
            vmem((4, 3, 96, 128), BF16),
            vmem((3, 3, 96, 128), BF16),
            vmem((8, 3, 24, 128), F32),
            vmem((7, 3, 24, 128), F32),
            vmem((4, 3, 32, WIDTH), BF16),
            vmem((3, 3, 32, WIDTH), BF16),
            vmem((4, 3, 48, 128), BF16),
            vmem((3, 3, 48, 128), BF16),
            dma((5,)), dma((4,)), dma((10 + 2 * len(PIECES),)), dma((10 + 2 * len(PIECES),)),
            dma((3, 3)), dma((3, 3)), dma((3, 2, 3)), dma((3, 2, 3)), dma((3, 3)), dma((3, 3)), dma((3, 7)), dma((3, 7)),
            dma((3, 3)), dma((3, 3)), dma((3, 2, 3)), dma((3, 2, 3)),
        ],
        compiler_params=pltpu.CompilerParams(
            collective_id=0, has_side_effects=True, vmem_limit_bytes=50 * 1024 * 1024
        ),
        cost_estimate=pl.CostEstimate(
            flops=18 * 2 * ROWS * WIDTH * WIDTH, bytes_accessed=10 * 1024 * 1024, transcendentals=2 * ROWS * WIDTH
        ),
    )(features, weights, cotangent)


def solution(mesh):
    in_specs = (P("dp", "seq", None), P(), P("dp", "seq", None))
    out_specs = (P("dp", "seq", None), P("dp", "seq", None), P(None, "seq", "dp"))
    return jax.shard_map(
        on_device, mesh=mesh, in_specs=in_specs, out_specs=out_specs, check_vma=False
    )
```

```python
import functools
import math

import jax
import jax.numpy as jnp
from jax import lax
from jax.experimental import pallas as pl
from jax.experimental.pallas import tpu as pltpu
from jax.sharding import PartitionSpec as P

MESH = pl.DeviceIdType.MESH
BF16 = jnp.bfloat16
F32 = jnp.float32
SEQS = 8
HALF = 64
WIDTH = 768
ROWS = SEQS * HALF
TILE = 256
TILES = WIDTH // TILE
ROOT = math.sqrt(2.0 / math.pi)
CUBIC = 0.044715
FACTOR = 1.0 / math.sqrt(64 * 4096)
PAIRS = ((0, 2), (3, 5), (1, 4))
CHUNKS = ((0, 1), (2,))
SLICES = (((0, 128), (256, 256), (640, 128)), ((128, 128), (512, 128)))
PIECES = ((0, 5), (5, 3))


def dot(a, b):
    return lax.dot_general(a, b, (((1,), (0,)), ((), ())), preferred_element_type=F32)


def dot_t(a, b):
    return lax.dot_general(a, b, (((1,), (1,)), ((), ())), preferred_element_type=F32)


def kernel(
    f_hbm, k_hbm, c_hbm, out_hbm, gin_hbm, wg_ref,
    f_v, c_v, k_v, a_v, at_v, d_v, c_halo, a_halo, conv, back, o_v, g_v,
    part, mate_part, ys, yr, xs, xr, zs, zr, xs2, xr2, ys2, yr2,
    in_sem, out_sem, halo_s, halo_r, core_s, core_r, y_s, y_r, x_s, x_r, z_s, z_r,
    y2_s, y2_r, x2_s, x2_r,
):
    s = lax.axis_index("seq")
    d = lax.axis_index("dp")
    core = lax.rem(s, 2)
    x = lax.rem(s // 2, 4)
    z_lo = s // 8
    y = d // 2
    z_hi = lax.rem(d, 2)
    z = z_hi * 4 + z_lo
    left = lax.rem(s + 31, 32)
    right = lax.rem(s + 1, 32)
    mate = s + 1 - 2 * core

    def y_partner(k):
        return {"seq": s, "dp": lax.rem(y + k, 4) * 2 + z_hi}

    def x_partner(k):
        return {"seq": (z_lo * 4 + lax.rem(x + k, 4)) * 2 + core, "dp": d}

    def z_partner(k):
        other = lax.rem(z + k, 8)
        return {"seq": (lax.rem(other, 4) * 4 + x) * 2 + core, "dp": y * 2 + other // 4}

    loads = []
    for half in range(2):
        rows = pl.ds(half * HALF, HALF)
        loads.append(pltpu.make_async_copy(f_hbm.at[:, rows, :], f_v.at[half], in_sem.at[half]))
    for half in range(2):
        rows = pl.ds(half * HALF, HALF)
        loads.append(pltpu.make_async_copy(c_hbm.at[:, rows, :], c_v.at[half], in_sem.at[2 + half]))
    loads.append(pltpu.make_async_copy(k_hbm, k_v, in_sem.at[4]))
    for load in loads:
        load.start()

    barrier = pltpu.get_barrier_semaphore()
    partners = [{"seq": left, "dp": d}, {"seq": right, "dp": d}]
    partners += [y_partner(k) for k in range(1, 4)]
    partners += [x_partner(k) for k in range(1, 4)]
    partners += [z_partner(k) for k in range(1, 8)]
    for partner in partners:
        pl.semaphore_signal(barrier, inc=1, device_id=partner, device_id_type=MESH)
    pl.semaphore_wait(barrier, len(partners))

    def remote(src, dst, send_sem, recv_sem, device):
        return pltpu.make_async_remote_copy(
            src_ref=src, dst_ref=dst, send_sem=send_sem, recv_sem=recv_sem,
            device_id=device, device_id_type=MESH,
        )

    def halo(i, src, dst, where):
        to_right = remote(src(1), dst.at[(0, *where)], halo_s.at[2 * i], halo_r.at[2 * i], {"seq": right, "dp": d})
        to_left = remote(src(0), dst.at[(1, *where)], halo_s.at[2 * i + 1], halo_r.at[2 * i + 1], {"seq": left, "dp": d})
        return to_right, to_left

    every = slice(None)
    cot_parts, act_parts = [], []
    for chunk in SLICES:
        cot_parts.append([(len(cot_parts) * 3 + i, (every, every, pl.ds(*cols))) for i, cols in enumerate(chunk)])
    for i, piece in enumerate(PIECES):
        act_parts.append([(5 + i, (pl.ds(*piece),))])
    cot_halo = [[halo(i, lambda half, p=p: c_v.at[(half, *p)], c_halo, p) for i, p in chunk] for chunk in cot_parts]
    act_halo = [[halo(i, lambda half, p=p: a_v.at[(half, *p)], a_halo, p) for i, p in chunk] for chunk in act_parts]

    def start_halo(chunk):
        @pl.when(s < 31)
        def _():
            for copies in chunk:
                copies[0].start()

        @pl.when(s > 0)
        def _():
            for copies in chunk:
                copies[1].start()

    def halo_into(i, dst, slot, where):
        return remote(
            dst.at[(0, *where)], dst.at[(slot, *where)], halo_s.at[2 * i], halo_r.at[2 * i + slot], {"seq": mate, "dp": d}
        )

    def receive_early(dst, parts):
        for i, where in parts:
            halo_into(i, dst, 1 - core, where).wait_recv()

    def receive_late(dst, parts):
        inside = jnp.logical_and(s > 0, s < 31)

        @pl.when(inside)
        def _():
            for i, where in parts:
                halo_into(i, dst, core, where).wait_recv()

        @pl.when(jnp.logical_not(inside))
        def _():
            for _, where in parts:
                blank = dst.at[(core, *where)]
                blank[...] = jnp.zeros(blank.shape, BF16)

    def sent_halo(copies):
        @pl.when(s < 31)
        def _():
            copies[0].wait_send()

        @pl.when(s > 0)
        def _():
            copies[1].wait_send()

    loads[2].wait()
    loads[3].wait()
    for chunk in cot_halo:
        start_halo(chunk)

    loads[0].wait()
    loads[1].wait()

    def activate(i, carry):
        half = i // 24
        pair = lax.rem(i // 6, 4)
        lanes = pl.ds(pl.multiple_of(lax.rem(i, 6) * 128, 128), 128)
        v = f_v[half, pl.ds(pair * 2, 2), :, lanes].reshape(128, 128).astype(F32)
        t = jnp.tanh(ROOT * v * (1.0 + CUBIC * (v * v)))
        act = v * (0.5 * (1.0 + t))
        a_v[half, pl.ds(pair * 2, 2), :, lanes] = act.astype(BF16).reshape(2, HALF, 128)
        rows = pl.ds(pl.multiple_of(pair * 128, 128), 128)
        at_v[half, lanes, rows] = act.T.astype(BF16)
        return carry

    lax.fori_loop(0, 48, activate, 0, unroll=2)

    def derive(i, carry):
        half = i // 24
        pair = lax.rem(i // 6, 4)
        lanes = pl.ds(pl.multiple_of(lax.rem(i, 6) * 128, 128), 128)
        v = f_v[half, pl.ds(pair * 2, 2), :, lanes].reshape(128, 128).astype(F32)
        sq = v * v
        t = jnp.tanh(ROOT * v * (1.0 + CUBIC * sq))
        slope = 0.5 * (1.0 + t) + 0.5 * v * (1.0 - t * t) * (ROOT * (1.0 + 3.0 * CUBIC * sq))
        d_v[half, pl.ds(pl.multiple_of(pair * 128, 128), 128), lanes] = slope
        return carry

    def cols_of(j):
        return pl.ds(pl.multiple_of(j * TILE, TILE), TILE)

    def cots(ref, half, j):
        tiles = [ref[half, :, :, t * 128 : t * 128 + 128].reshape(ROWS, 128) for t in PAIRS[j]]
        return jnp.concatenate(tiles, axis=1)

    def rows_of(ref, half):
        return ref[half].reshape(ROWS, WIDTH)

    def core_copy(tap, j):
        return remote(
            part.at[tap, j, :, :, 1 - core], mate_part.at[tap, j], core_s.at[tap, j], core_r.at[tap, j],
            {"seq": mate, "dp": d},
        )

    def grad_terms(tap, terms, add, send, tiles=range(TILES)):
        for j in tiles:
            total = dot(at_v[terms[0][0]], cots(terms[0][1], terms[0][2], j))
            for act_half, ref, half in terms[1:]:
                total = total + dot(at_v[act_half], cots(ref, half, j))
            total = total.reshape(4, 4, 2, 24, TILE)
            if add:
                total = total + part[tap, j]
            part[tap, j] = total
            if send:
                core_copy(tap, j).start()

    def y_copy(tap, chunk):
        rows = pl.ds(64 * chunk, 64 - 32 * chunk)
        return [
            remote(
                ys.at[lax.rem(y + k, 4), tap, :, rows], yr.at[k - 1, tap, :, rows],
                y_s.at[tap, chunk, k - 1], y_r.at[tap, chunk, k - 1], y_partner(k),
            )
            for k in range(1, 4)
        ]

    def x_copy(tap):
        return [
        remote(xs.at[lax.rem(x + k, 4), tap], xr.at[k - 1, tap], x_s.at[tap, k - 1], x_r.at[tap, k - 1], x_partner(k))
        for k in range(1, 4)
        ]

    def z_copy(tap):
        return [
        remote(zs.at[lax.rem(z + k, 8), tap], zr.at[k - 1, tap], z_s.at[tap, k - 1], z_r.at[tap, k - 1], z_partner(k))
        for k in range(1, 8)
        ]


    def x_first(tap, chunk):
        cols = pl.ds(512 * chunk, 512 - 256 * chunk)
        return [
            remote(
                xs2.at[lax.rem(x + k, 4), tap, :, cols], xr2.at[k - 1, tap, :, cols],
                x2_s.at[tap, chunk, k - 1], x2_r.at[tap, chunk, k - 1], x_partner(k),
            )
            for k in range(1, 4)
        ]

    def y_second(tap):
        return [
        remote(ys2.at[lax.rem(y + k, 4), tap], yr2.at[k - 1, tap], y2_s.at[tap, k - 1], y2_r.at[tap, k - 1], y_partner(k))
        for k in range(1, 4)
        ]

    lane16 = lax.broadcasted_iota(jnp.int32, (16, 128), 1)
    lane32 = lax.broadcasted_iota(jnp.int32, (32, 128), 1)
    lane96 = lax.broadcasted_iota(jnp.int32, (96, 128), 1)

    def packed_for(to, shared, lane):
        a, b = shared[: lane.shape[0]], shared[lane.shape[0] :]
        if to % 2 == 0:
            return jnp.where(lane < 64, a, pltpu.roll(b, 64, 1))
        return jnp.where(lane < 64, pltpu.roll(a, 64, 1), b)

    def send_y(tap, chunk):
        def body(i, carry):
            for j in CHUNKS[chunk]:
                total = part[tap, j, :, i, core, :16] + mate_part[tap, j, :, i, :16]
                total = total.reshape(64, TILE)
                tiles = total[:, :128], total[:, 128:]
                if chunk == 0:
                    for half in range(2):
                        ys[2 * j + half, tap, i, :64] = tiles[half].astype(BF16)
                else:
                    for to in range(4):
                        ys[to, tap, i, 64:] = packed_for(to, tiles[to // 2], lane32).astype(BF16)
            return carry

        lax.fori_loop(0, 4, body, 0)
        for copy in y_copy(tap, chunk):
            copy.start()

    def send_x_first(tap, chunk):
        def body(i, carry):
            for j in CHUNKS[chunk]:
                total = part[tap, j, :, i, core, 16:] + mate_part[tap, j, :, i, 16:]
                xs2[i, tap, :, j * TILE : (j + 1) * TILE] = total.reshape(32, TILE).astype(BF16)
            return carry

        lax.fori_loop(0, 4, body, 0)
        for copy in x_first(tap, chunk):
            copy.start()

    def send_y_second(tap):
        for copy in x_first(tap, 0) + x_first(tap, 1):
            copy.wait_recv()
        tiles = []
        for j in range(6):
            cols = slice(j * 128, j * 128 + 128)
            total = xs2[x, tap, :, cols].astype(F32)
            for k in range(3):
                total = total + xr2[k, tap, :, cols].astype(F32)
            tiles.append(total)
        for to in range(4):
            ys2[to, tap, :32] = tiles[to].astype(BF16)
            ys2[to, tap, 32:] = packed_for(to, tiles[4 + to // 2], lane16).astype(BF16)
        for copy in y_second(tap):
            copy.start()

    def send_first(tap, chunk):
        for j in CHUNKS[chunk]:
            core_copy(tap, j).wait_recv()
        send_y(tap, chunk)
        send_x_first(tap, chunk)

    def send_x(tap):
        for copy in y_copy(tap, 0) + y_copy(tap, 1):
            copy.wait_recv()

        def body(i, carry):
            total = ys[y, tap, i].astype(F32)
            for k in range(3):
                total = total + yr[k, tap, i].astype(F32)
            xs[i, tap] = total.astype(BF16)
            return carry

        lax.fori_loop(0, 4, body, 0)
        for copy in x_copy(tap):
            copy.start()

    def send_z(tap):
        for copy in x_copy(tap) + y_second(tap):
            copy.wait_recv()

        def gathered(own, others, rows):
            total = own.astype(F32)
            for k in range(3):
                total = total + others[k, tap].astype(F32)
            packed = total[4 * rows :]
            rest = jnp.concatenate([packed, pltpu.roll(packed, 64, 1)], axis=0)
            return total[: 4 * rows].reshape(4, rows, 128), rest.reshape(4, rows, 128)

        full_a, rest_a = gathered(xs[x, tap], xr, 16)
        full_b, rest_b = gathered(ys2[y, tap], yr2, 8)
        full = jnp.concatenate([full_a, full_b], axis=1).reshape(96, 128)
        rest = jnp.concatenate([rest_a, rest_b], axis=1).reshape(96, 128)
        odd = lax.rem(y, 2) == 1
        first = jnp.where(odd, jnp.where(lane96 < 64, rest, pltpu.roll(full, 64, 1)), full)
        second = jnp.where(odd, pltpu.roll(full, 96, 1), pltpu.roll(jnp.where(lane96 >= 96, full, rest), 32, 1))
        zs[0:4, tap] = first.reshape(4, 24, 128)
        zs[4:8, tap] = second.reshape(4, 24, 128)
        for copy in z_copy(tap):
            copy.start()

    def conv_inner(j, carry):
        cols = cols_of(j)
        head, tail = rows_of(a_v, 0), rows_of(a_v, 1)
        conv[0, :, cols] = dot(head, k_v[1, :, cols]) + dot(tail, k_v[2, :, cols])
        conv[1, :, cols] = dot(head, k_v[0, :, cols]) + dot(tail, k_v[1, :, cols])
        return carry

    def back_inner(j, carry):
        cols = cols_of(j)
        head, tail = rows_of(c_v, 0), rows_of(c_v, 1)
        back[0, :, cols] = dot_t(tail, k_v[0, cols, :]) + dot_t(head, k_v[1, cols, :])
        back[1, :, cols] = dot_t(tail, k_v[1, cols, :]) + dot_t(head, k_v[2, cols, :])
        return carry

    def back_outer(j, carry):
        cols = cols_of(j)
        for half, tap in ((0, 2), (1, 0)):
            total = back[half, :, cols] + dot_t(rows_of(c_halo, half), k_v[tap, cols, :])
            own = c_v[half, :, :, cols].reshape(ROWS, TILE).astype(F32)
            result = own + d_v[half, :, cols] * total
            g_v[half, :, :, cols] = result.astype(BF16).reshape(SEQS, HALF, TILE)
        return carry

    def conv_outer(j, carry):
        cols = cols_of(j)
        for half, tap in ((0, 0), (1, 2)):
            total = conv[half, :, cols] + dot(rows_of(a_halo, half), k_v[tap, :, cols])
            own = f_v[half, :, :, cols].reshape(ROWS, TILE).astype(F32)
            o_v[half, :, :, cols] = (own + total).astype(BF16).reshape(SEQS, HALF, TILE)
        return carry

    stores = []

    def store(i, source, target):
        for half in range(2):
            rows = pl.ds(half * HALF, HALF)
            stores.append(pltpu.make_async_copy(source.at[half], target.at[:, rows, :], out_sem.at[2 * i + half]))
            stores[-1].start()

    early, late = 2 * core, 2 - 2 * core

    def grad_outer(tap, half, chunk):
        grad_terms(tap, [(half, c_halo, half)], True, True, CHUNKS[chunk])

    grad_terms(1, [(0, c_v, 0), (1, c_v, 1)], False, True)
    grad_terms(0, [(0, c_v, 1)], False, False)
    grad_terms(2, [(1, c_v, 0)], False, False)
    send_first(1, 0)
    send_first(1, 1)
    for chunk in range(2):
        receive_early(c_halo, cot_parts[chunk])
        grad_outer(early, 1 - core, chunk)
    loads[4].wait()
    for chunk in range(2):
        receive_late(c_halo, cot_parts[chunk])
        if chunk == 1:
            start_halo(act_halo[0])
        grad_outer(late, core, chunk)
        send_first(late, chunk)
        send_first(early, chunk)
    send_x(1)
    send_y_second(1)
    lax.fori_loop(0, TILES, back_inner, 0)
    lax.fori_loop(0, 48, derive, 0, unroll=2)
    send_x(late)
    send_y_second(late)
    send_x(early)
    send_y_second(early)
    start_halo(act_halo[1])
    send_z(1)
    lax.fori_loop(0, TILES, back_outer, 0)
    store(0, g_v, gin_hbm)
    send_z(late)
    send_z(early)
    lax.fori_loop(0, TILES, conv_inner, 0)
    for parts in act_parts:
        receive_early(a_halo, parts)
        receive_late(a_halo, parts)
    lax.fori_loop(0, TILES, conv_outer, 0)
    store(1, o_v, out_hbm)
    for chunk in cot_halo + act_halo:
        for copies in chunk:
            sent_halo(copies)
    for tap in range(3):
        for j in range(TILES):
            core_copy(tap, j).wait_send()
        for copy in y_copy(tap, 0) + y_copy(tap, 1) + x_first(tap, 0) + x_first(tap, 1):
            copy.wait_send()
        for copy in x_copy(tap) + y_second(tap):
            copy.wait_send()
    for tap in (1, late, early):
        for copy in z_copy(tap):
            copy.wait_recv()
        total = zs[z, tap]
        for k in range(7):
            total = total + zr[k, tap]
        wg_ref[tap] = (total * FACTOR)[:, :96]

    for tap in range(3):
        for copy in z_copy(tap):
            copy.wait_send()
    for pending in stores:
        pending.wait()


def on_device(features, weights, cotangent):
    block = jax.ShapeDtypeStruct(features.shape, BF16)
    hbm = pl.BlockSpec(memory_space=pl.ANY)
    vmem = pltpu.VMEM
    dma = pltpu.SemaphoreType.DMA
    halves = (2, SEQS, HALF, WIDTH)
    return pl.pallas_call(
        kernel,
        out_shape=(block, block, jax.ShapeDtypeStruct((3, 24, 96), F32)),
        in_specs=[hbm, hbm, hbm],
        out_specs=(hbm, hbm, pl.BlockSpec(memory_space=pltpu.VMEM)),
        scratch_shapes=[
            vmem(halves, BF16),
            vmem(halves, BF16),
            vmem((3, WIDTH, WIDTH), BF16),
            vmem(halves, BF16),
            vmem((2, WIDTH, ROWS), BF16),
            vmem((2, ROWS, WIDTH), F32),
            vmem(halves, BF16),
            vmem(halves, BF16),
            vmem((2, ROWS, WIDTH), F32),
            vmem((2, ROWS, WIDTH), F32),
            vmem(halves, BF16),
            vmem(halves, BF16),
            vmem((3, TILES, 4, 4, 2, 24, TILE), F32),
            vmem((3, TILES, 4, 4, 24, TILE), F32),
            vmem((4, 3, 4, 96, 128), BF16),
            vmem((3, 3, 4, 96, 128), BF16),
            vmem((4, 3, 96, 128), BF16),
            vmem((3, 3, 96, 128), BF16),
            vmem((8, 3, 24, 128), F32),
            vmem((7, 3, 24, 128), F32),
            vmem((4, 3, 32, WIDTH), BF16),
            vmem((3, 3, 32, WIDTH), BF16),
            vmem((4, 3, 48, 128), BF16),
            vmem((3, 3, 48, 128), BF16),
            dma((5,)), dma((4,)), dma((10 + 2 * len(PIECES),)), dma((10 + 2 * len(PIECES),)),
            dma((3, 3)), dma((3, 3)), dma((3, 2, 3)), dma((3, 2, 3)), dma((3, 3)), dma((3, 3)), dma((3, 7)), dma((3, 7)),
            dma((3, 3)), dma((3, 3)), dma((3, 2, 3)), dma((3, 2, 3)),
        ],
        compiler_params=pltpu.CompilerParams(
            collective_id=0, has_side_effects=True, vmem_limit_bytes=50 * 1024 * 1024
        ),
        cost_estimate=pl.CostEstimate(
            flops=18 * 2 * ROWS * WIDTH * WIDTH, bytes_accessed=10 * 1024 * 1024, transcendentals=2 * ROWS * WIDTH
        ),
    )(features, weights, cotangent)


def solution(mesh):
    in_specs = (P("dp", "seq", None), P(), P("dp", "seq", None))
    out_specs = (P("dp", "seq", None), P("dp", "seq", None), P(None, "seq", "dp"))
    return jax.shard_map(
        on_device, mesh=mesh, in_specs=in_specs, out_specs=out_specs, check_vma=False
    )
```
